128 devices in a mesh: gy: 16 (over y_lo, x, core), gx: 8 (over z, y_hi).
Axes of the slice: x: 4, y: 4 (y_hi: 2, y_lo: 2; y = y_hi * 2 + y_lo), z: 4, core: 2. Of those that a mesh axis runs over, the one named last changes fastest.
Arguments:
- tokens: bfloat16 [8, 128, 256, 192], P(None, 'gy', 'gx'), may hold values from -6 to 6
- cotangent: bfloat16 [8, 128, 256, 192], P(None, 'gy', 'gx'), may hold values from -3 to 3
- gains: float32 [2, 192], replicated, may hold values from 0.1 to 1.9
- qkv_weight: bfloat16 [2, 192, 576], replicated, may hold values from -1.4433757 to 1.4433757, as said below
- proj_weight: bfloat16 [2, 192, 192], replicated, may hold values from -0.4375 to 0.4375
Outputs:
- grad_tokens: float32 [8, 128, 256, 192], P(None, 'gy', 'gx')
- grad_gains: float32 [2, 192], replicated
- grad_qkv: float32 [2, 192, 576], replicated
- grad_proj: float32 [2, 192, 192], replicated
The draws below stay inside these ranges and needn't reach their ends.
Inputs may be any that keep to these rules, and one draw needn't show every extreme that they name: `qkv_weight`: the last dimension holds the query, key and value projections in that order.
All inputs are finite; a program needn't handle non-finite values.
Results may differ from the reference program's by a relative error of at most 0.02.
The reference program's roundings to bfloat16 on the way count: a program that leaves them out, or rounds other values in their place, can miss the bound.
Values may be sent and summed in bfloat16 or wider, within the bound.
A program may use at most 128 MiB of HBM per device.

```python
import jax
import jax.numpy as jnp
from jax import lax

C = 192
HEADS = 6
WIN = 8
DEPTH = 8
NY = 128
NX = 256
TOKENS = 262144


def draw_qkv_weight(key, part):
    key = jax.random.fold_in(key, 11)
    base = jnp.clip(jax.random.normal(key, (2, C, 3 * C), jnp.float32), -4.0, 4.0) * C ** (-0.5)
    return base.astype(jnp.bfloat16)


def level_of(stream_key, shape, cuts, smallest, high):
    def one(dim, shards_of):
        steps = jax.random.uniform(jax.random.fold_in(jax.random.fold_in(stream_key, 6), dim), (shards_of,), jnp.float32, smallest / len(cuts), high / len(cuts))
        return jnp.repeat(jnp.exp(steps), shape[dim] // shards_of).reshape((-1,) + (1,) * (len(shape) - dim - 1))

    level = one(*cuts[0])
    for cut in cuts[1:]:
        level = level * one(*cut)
    return level


def scatter_about(rng, dims, spread, most, cuts=(), held_as=jnp.bfloat16):
    values = jax.random.normal(rng, dims, jnp.float32) * spread
    if len(cuts) > 0:
        values = level_of(rng, dims, cuts, -0.22, 0.18) * values
    return jnp.clip(values, min=-most, max=most).astype(held_as)


def setup_inputs(seed: int = 0) -> dict:
    arg_keys = jax.random.split(jax.random.key(seed), 6)
    tokens = scatter_about(arg_keys[0], (DEPTH, NY, NX, C), 1.0, 6.0, ((1, 16), (2, 8)))
    cotangent = scatter_about(arg_keys[1], (DEPTH, NY, NX, C), 1.0, 3.0, ((1, 16), (2, 8)))
    gains = jnp.clip(1.0 + 0.18 * jax.random.normal(arg_keys[2], (2, C), jnp.float32), 0.1, 1.9)
    qkv_weight = draw_qkv_weight(jax.random.fold_in(arg_keys[5], 71), 0)
    proj_weight = scatter_about(arg_keys[4], (2, C, C), C ** -0.5, 0.4375)
    return dict(tokens=tokens, cotangent=cotangent, gains=gains, qkv_weight=qkv_weight, proj_weight=proj_weight)


EPSILON = 1e-05
MASKED = -1e+30

def windows_of(cells, window_size):
    depth_count, row_count, col_count, features = cells.shape
    blocks = cells.reshape(depth_count // window_size, window_size, row_count // window_size, window_size, col_count // window_size, window_size, features)
    blocks = blocks.transpose(0, 2, 4, 1, 3, 5, 6)
    return blocks.reshape(-1, window_size ** 3, features)

def cells_of(blocks, depth_count, row_count, col_count, window_size):
    features = blocks.shape[-1]
    cells = blocks.reshape(depth_count // window_size, row_count // window_size, col_count // window_size, window_size, window_size, window_size, features)
    cells = cells.transpose(0, 3, 1, 4, 2, 5, 6)
    return cells.reshape(depth_count, row_count, col_count, features)

def normalize(cells, gain_row):
    values = cells.astype(jnp.float32)
    center = values - lax.optimization_barrier(jnp.mean(values, axis=-1, keepdims=True))
    inverse = lax.rsqrt(lax.optimization_barrier(jnp.mean(center * center, axis=-1, keepdims=True)) + EPSILON)
    normed = center * inverse
    return ((normed * gain_row).astype(jnp.bfloat16), normed, inverse)

def norm_back(d_normed, normed, inverse, gain_row):
    scaled = d_normed * gain_row
    mean_first = lax.optimization_barrier(jnp.mean(scaled, axis=-1, keepdims=True))
    mean_second = lax.optimization_barrier(jnp.mean(scaled * normed, axis=-1, keepdims=True))
    return inverse * (scaled - mean_first - normed * mean_second)

def region(position, extent, window_size):
    return (position >= extent - window_size).astype(jnp.int32) + (position >= extent - window_size // 2).astype(jnp.int32)

def product(form, left, right):
    return jnp.einsum(form, left.astype(jnp.float32), right.astype(jnp.float32), precision=lax.Precision.HIGHEST)

def attention_weights(query_rows, key_rows, region_ids, scale):
    scores = product('qhd,khd->hqk', query_rows, key_rows) * scale
    allowed = region_ids[:, None] == region_ids[None, :]
    scores = jnp.where(allowed[None], scores, MASKED)
    row_max = lax.optimization_barrier(jnp.max(scores, axis=-1, keepdims=True))
    powers = jnp.exp(scores - row_max)
    return powers / lax.optimization_barrier(jnp.sum(powers, axis=-1, keepdims=True))

def window_forward(packed, region_ids):
    split = packed.reshape(packed.shape[0], 3, HEADS, -1)
    scale = split.shape[-1] ** (-0.5)
    weights = attention_weights(split[:, 0], split[:, 1], region_ids, scale)
    rounded = weights.astype(jnp.bfloat16)
    attended = product('hqk,khd->qhd', rounded, split[:, 2])
    return attended.astype(jnp.bfloat16).reshape(packed.shape[0], -1)

def window_backward(packed, region_ids, d_attended):
    split = packed.reshape(packed.shape[0], 3, HEADS, -1)
    scale = split.shape[-1] ** (-0.5)
    query_rows, key_rows, value_rows = (split[:, 0], split[:, 1], split[:, 2])
    weights = attention_weights(query_rows, key_rows, region_ids, scale)
    rounded = weights.astype(jnp.bfloat16)
    d_output = d_attended.reshape(query_rows.shape)
    d_weights = product('qhd,khd->hqk', d_output, value_rows)
    d_values = product('hqk,qhd->khd', rounded, d_output)
    d_scores = weights * (d_weights - lax.optimization_barrier(jnp.sum(d_weights * weights, axis=-1, keepdims=True)))
    d_scaled = (d_scores * scale).astype(jnp.bfloat16)
    d_query = product('hqk,khd->qhd', d_scaled, key_rows)
    d_keys = product('hqk,qhd->khd', d_scaled, query_rows)
    stacked = jnp.stack([d_query, d_keys, d_values], axis=1)
    return stacked.astype(jnp.bfloat16).reshape(packed.shape[0], -1)

def grouped_map(function, arrays, group):
    count = arrays[0].shape[0]
    grouped = tuple((part.reshape((count // group, group) + part.shape[1:]) for part in arrays))
    result = lax.map(lambda window_batch: jax.vmap(function)(*window_batch), grouped)
    return result.reshape((count,) + result.shape[2:])

def block_forward(cells, gain_row, qkv_matrix, id_cells):
    depth_count, row_count, col_count, features = cells.shape
    normed_b, normed, inverse = normalize(cells, gain_row)
    packed = jnp.dot(normed_b.reshape(-1, features), qkv_matrix, preferred_element_type=jnp.float32).astype(jnp.bfloat16)
    packed_win = windows_of(packed.reshape(depth_count, row_count, col_count, -1), WIN)
    ids_win = windows_of(id_cells, WIN)[..., 0]
    attended_win = grouped_map(window_forward, (packed_win, ids_win), NX // WIN)
    attended = cells_of(attended_win, depth_count, row_count, col_count, WIN).reshape(-1, features)
    return (normed_b, normed, inverse, packed_win, ids_win, attended)

def block_backward(state, cot_cells, qkv_matrix, proj_matrix):
    normed_b, normed, inverse, packed_win, ids_win, attended = state
    depth_count, row_count, col_count, features = cot_cells.shape
    cot_flat = cot_cells.reshape(-1, features)
    d_attended = jnp.dot(cot_flat, proj_matrix.T, preferred_element_type=jnp.float32).astype(jnp.bfloat16)
    proj_sum = jnp.dot(attended.T, cot_flat, preferred_element_type=jnp.float32)
    d_att_win = windows_of(d_attended.reshape(depth_count, row_count, col_count, features), WIN)
    d_packed_win = grouped_map(window_backward, (packed_win, ids_win, d_att_win), NX // WIN)
    d_packed = cells_of(d_packed_win, depth_count, row_count, col_count, WIN).reshape(-1, 3 * features)
    qkv_sum = jnp.dot(normed_b.reshape(-1, features).T, d_packed, preferred_element_type=jnp.float32)
    d_normed = jnp.dot(d_packed, qkv_matrix.T, preferred_element_type=jnp.float32).reshape(depth_count, row_count, col_count, features)
    gain_sum = lax.optimization_barrier(jnp.sum(d_normed * normed, axis=(0, 1, 2)))
    return (d_normed, gain_sum, qkv_sum, proj_sum)

def reference(tokens, cotangent, gains, qkv_weight, proj_weight):
    half_span = WIN // 2
    depth_pos = jnp.arange(DEPTH, dtype=jnp.int32)
    row_pos = jnp.arange(NY, dtype=jnp.int32)
    col_pos = jnp.arange(NX, dtype=jnp.int32)
    shifted_ids = (9 * region(depth_pos, DEPTH, WIN)[:, None, None] + 3 * region(row_pos, NY, WIN)[None, :, None] + region(col_pos, NX, WIN)[None, None, :])[..., None]
    zero_ids = jnp.zeros((DEPTH, NY, NX, 1), jnp.int32)
    state_zero = block_forward(tokens, gains[0], qkv_weight[0], zero_ids)
    branch = jnp.dot(state_zero[5], proj_weight[0], preferred_element_type=jnp.float32).reshape(tokens.shape)
    middle = (tokens.astype(jnp.float32) + branch).astype(jnp.bfloat16)
    moved = jnp.roll(middle, (-half_span, -half_span, -half_span), axis=(0, 1, 2))
    cot_moved = jnp.roll(cotangent, (-half_span, -half_span, -half_span), axis=(0, 1, 2))
    state_one = block_forward(moved, gains[1], qkv_weight[1], shifted_ids)
    d_normed_one, gain_one, qkv_one, proj_one = block_backward(state_one, cot_moved, qkv_weight[1], proj_weight[1])
    d_branch_one = norm_back(d_normed_one, state_one[1], state_one[2], gains[1])
    grad_mid = (cotangent.astype(jnp.float32) + jnp.roll(d_branch_one, (half_span, half_span, half_span), axis=(0, 1, 2))).astype(jnp.bfloat16)
    d_normed_zero, gain_zero, qkv_zero, proj_zero = block_backward(state_zero, grad_mid, qkv_weight[0], proj_weight[0])
    d_branch_zero = norm_back(d_normed_zero, state_zero[1], state_zero[2], gains[0])
    grad_tokens = grad_mid.astype(jnp.float32) + d_branch_zero
    factor = (TOKENS // 16) ** (-0.5)
    grad_gains = jnp.stack([gain_zero, gain_one]) * factor
    grad_qkv = jnp.stack([qkv_zero, qkv_one]) * factor
    grad_proj = jnp.stack([proj_zero, proj_one]) * factor
    return (grad_tokens, grad_gains, grad_qkv, grad_proj)
```

```python
import functools
import math

import jax
import jax.numpy as jnp
from jax import lax
from jax.experimental import pallas as pl
from jax.experimental.pallas import tpu as pltpu
from jax.sharding import PartitionSpec as P

HEADS = 6
WIN = 8
C = 192
HD = 32
TOK = WIN**3
HALF = TOK // 2
EPSILON = 1e-05
MASKED = -1e30
SCALE = HD**-0.5
LOG2E = 1.0 / math.log(2.0)
LN2 = math.log(2.0)
F32 = jnp.float32
BF16 = jnp.bfloat16
GROUPS = ((0, 1, 2), (3, 4, 5))


def dot(left, right):
    return jnp.dot(left, right, preferred_element_type=F32)


def dot_t(left, right):
    return lax.dot_general(left, right, (((1,), (1,)), ((), ())), preferred_element_type=F32)


def rows(head, part=0):
    start = part * C + head * HD
    return slice(start, start + HD)


def layer_norm(x, gain_row):
    center = x - jnp.sum(x, axis=-1, keepdims=True) * (1.0 / C)
    inverse = lax.rsqrt(jnp.sum(center * center, axis=-1, keepdims=True) * (1.0 / C) + EPSILON)
    normed = center * inverse
    return (normed * gain_row).astype(BF16), normed, inverse


def norm_back(d_normed, normed, inverse, gain_row):
    scaled = d_normed * gain_row
    first = jnp.sum(scaled, axis=-1, keepdims=True) * (1.0 / C)
    second = jnp.sum(scaled * normed, axis=-1, keepdims=True) * (1.0 / C)
    return inverse * (scaled - first - normed * second)


def fold_tokens(x):
    return jnp.sum(x.reshape(TOK // 8, 8, C), axis=0)


def halves(first, second):
    a = first.astype(F32).reshape(TOK // 8, 8, C)
    b = second.astype(F32).reshape(TOK // 8, 8, C)
    place = lax.broadcasted_iota(jnp.int32, (TOK // 8, 8, C), 1)
    return jnp.where(place < 4, a, b).reshape(TOK, C)


def prepare_weights(block, w_ref, p_ref, wt_ref, wkv_ref, pt_ref):
    weight = w_ref[block].astype(F32)
    wt_ref[...] = weight.T.astype(BF16)
    wkv_ref[...] = weight[:, C:].astype(BF16)
    if pt_ref is not None:
        pt_ref[...] = p_ref[block].astype(F32).T.astype(BF16)


def project(normed_b, wt_ref, wkv_ref, qkvt_ref, kv_ref):
    qkvt_ref[:C] = (dot_t(wt_ref[:C], normed_b) * (SCALE * LOG2E)).astype(BF16)
    qkvt_ref[C:] = dot_t(wt_ref[C:], normed_b).astype(BF16)
    kv_ref[...] = dot(normed_b, wkv_ref[...]).astype(BF16)


def regular_forward(group, qkvt_ref, kv_ref, e_ref, r_ref, o_ref):
    s = [dot(kv_ref[:, rows(h)], qkvt_ref[rows(h)]) for h in group]
    m = [jnp.max(x, axis=0, keepdims=True) for x in s]
    ef = [jnp.exp2(x - y) for x, y in zip(s, m)]
    e = [x.astype(BF16) for x in ef]
    for h, x in zip(group, e):
        e_ref[h] = x
    r = [1.0 / jnp.sum(x, axis=0, keepdims=True) for x in ef]
    o = [dot(qkvt_ref[rows(h, 2)], x) for h, x in zip(group, e)]
    for h, x, y in zip(group, o, r):
        o_ref[rows(h)] = x * y
        r_ref[h : h + 1] = y


def regular_backward(group, qkvt_ref, kv_ref, e_ref, r_ref, o_ref, da_ref, dqkvt_ref):
    da = [(da_ref[rows(h)] * r_ref[h : h + 1]).astype(BF16) for h in group]
    d = [
        jnp.sum(x.astype(F32) * o_ref[rows(h)], axis=0, keepdims=True) for h, x in zip(group, da)
    ]
    dp = [dot(kv_ref[:, rows(h, 1)], x) for h, x in zip(group, da)]
    for h, x in zip(group, da):
        dqkvt_ref[rows(h, 2)] = dot_t(x, e_ref[h]).astype(BF16)
    ds = [
        (e_ref[h].astype(F32) * (x - y)).astype(BF16) for h, x, y in zip(group, dp, d)
    ]
    for h, x in zip(group, ds):
        dqkvt_ref[rows(h)] = (dot(qkvt_ref[rows(h, 1)], x) * SCALE).astype(BF16)
        dqkvt_ref[rows(h, 1)] = (dot_t(qkvt_ref[rows(h)], x) * LN2).astype(BF16)


def shifted_both(group, qkvt_ref, kv_ref, bias, o_ref, da_ref, dqkvt_ref):
    parts = [(h, slice(k * HALF, (k + 1) * HALF)) for h in group for k in range(2)]
    s = [dot(kv_ref[t, rows(h)], qkvt_ref[rows(h), t]) + bias for h, t in parts]
    m = [jnp.max(x, axis=0, keepdims=True) for x in s]
    ef = [jnp.exp2(x - y) for x, y in zip(s, m)]
    e = [x.astype(BF16) for x in ef]
    r = [1.0 / jnp.sum(x, axis=0, keepdims=True) for x in ef]
    o = [dot(qkvt_ref[rows(h, 2), t], x) * y for (h, t), x, y in zip(parts, e, r)]
    da = [(da_ref[rows(h), t] * y).astype(BF16) for (h, t), y in zip(parts, r)]
    d = [jnp.sum(x.astype(F32) * y, axis=0, keepdims=True) for x, y in zip(da, o)]
    dp = [dot(kv_ref[t, rows(h, 1)], x) for (h, t), x in zip(parts, da)]
    for (h, t), x, y, z in zip(parts, o, da, e):
        o_ref[rows(h), t] = x.astype(BF16)
        dqkvt_ref[rows(h, 2), t] = dot_t(y, z).astype(BF16)
    ds = [(x.astype(F32) * (y - z)).astype(BF16) for x, y, z in zip(e, dp, d)]
    for (h, t), x in zip(parts, ds):
        dqkvt_ref[rows(h), t] = (dot(qkvt_ref[rows(h, 1), t], x) * SCALE).astype(BF16)
        dqkvt_ref[rows(h, 1), t] = (dot_t(qkvt_ref[rows(h), t], x) * LN2).astype(BF16)


def write_bias(bias_ref):
    last_row = lax.axis_index("gy") == lax.axis_size("gy") - 1
    last_col = lax.axis_index("gx") == lax.axis_size("gx") - 1
    key = lax.broadcasted_iota(jnp.int32, (HALF, HALF), 0)
    query = lax.broadcasted_iota(jnp.int32, (HALF, HALF), 1)
    row_bias = jnp.where((key // 32) % 2 != (query // 32) % 2, MASKED, 0.0).astype(F32)
    col_bias = jnp.where((key // 4) % 2 != (query // 4) % 2, MASKED, 0.0).astype(F32)
    row_bias = row_bias * jnp.where(last_row, 1.0, 0.0).astype(F32)
    col_bias = col_bias * jnp.where(last_col, 1.0, 0.0).astype(F32)
    bias_ref[0] = row_bias
    bias_ref[1] = jnp.minimum(row_bias, col_bias)


def kernel_forward(
    tok_ref, gain_ref, w_ref, p_ref,
    mid_ref, e_ref, r_ref, o_ref, qkvt_ref, kv_ref, nb_ref, normed_ref, inv_ref,
    x32_ref, wt_ref, wkv_ref, pt_ref,
):
    prepare_weights(0, w_ref, p_ref, wt_ref, wkv_ref, pt_ref)
    x32_ref[...] = tok_ref[...].astype(F32)

    def window(w, carry):
        x = x32_ref[:, :, pl.ds(pl.multiple_of(w * WIN, WIN), WIN), :].reshape(TOK, C)
        normed_b, normed, inverse = layer_norm(x, gain_ref[0:1])
        nb_ref[w] = normed_b
        normed_ref[w] = normed
        inv_ref[w] = inverse
        project(normed_b, wt_ref, wkv_ref, qkvt_ref.at[w], kv_ref.at[w])
        for group in GROUPS:
            regular_forward(
                group, qkvt_ref.at[w], kv_ref.at[w], e_ref.at[w], r_ref.at[w], o_ref.at[w]
            )
        branch = dot(pt_ref[...], o_ref[w].astype(BF16)).T
        mid_ref[w] = (x + branch).astype(BF16).reshape(WIN, 64, C)
        return carry

    lax.fori_loop(0, 4, window, 0)


def kernel_shifted(
    mid_ref, cot_ref, gain_ref, w_ref, p_ref,
    grad_ref, wsum_ref, gsum_ref,
    qkvt_ref, kv_ref, o_ref, da_ref, dqkvt_ref, bias_ref, wt_ref, wkv_ref,
):
    prepare_weights(1, w_ref, p_ref, wt_ref, wkv_ref, None)
    write_bias(bias_ref)
    wsum_ref[...] = jnp.zeros_like(wsum_ref)
    gsum_ref[...] = jnp.zeros_like(gsum_ref)

    def window(w, carry):
        x = halves(mid_ref[w + 1], mid_ref[w])
        normed_b, normed, inverse = layer_norm(x, gain_ref[1:2])
        project(normed_b, wt_ref, wkv_ref, qkvt_ref, kv_ref)
        cot = halves(cot_ref[w + 1], cot_ref[w])
        cot_b = cot.astype(BF16)
        da_ref[...] = dot_t(p_ref[1], cot_b)
        bias = bias_ref[w // 3]
        for group in GROUPS:
            shifted_both(group, qkvt_ref, kv_ref, bias, o_ref, da_ref, dqkvt_ref)
        wsum_ref[3 * C :] += dot(o_ref[...], cot_b)
        wsum_ref[: 3 * C] += dot(dqkvt_ref[...], normed_b)
        d_normed = dot(w_ref[1], dqkvt_ref[...]).T
        gsum_ref[...] += fold_tokens(d_normed * normed)
        grad = cot + norm_back(d_normed, normed, inverse, gain_ref[1:2])
        grad_ref[w] = grad.astype(BF16).reshape(WIN, 64, C)
        return carry

    lax.fori_loop(0, 4, window, 0)


def kernel_backward(
    grad_ref, gain_ref, w_ref, p_ref, e_ref, r_ref, o_ref, qkvt_ref, kv_ref, nb_ref, normed_ref, inv_ref,
    out_ref, wsum_ref, gsum_ref,
    da_ref, dqkvt_ref,
):
    wsum_ref[...] = jnp.zeros_like(wsum_ref)
    gsum_ref[...] = jnp.zeros_like(gsum_ref)

    def window(w, carry):
        grad = halves(grad_ref[w], grad_ref[w + 1])
        grad_b = grad.astype(BF16)
        da_ref[...] = dot_t(p_ref[0], grad_b)
        for group in GROUPS:
            regular_backward(
                group, qkvt_ref.at[w], kv_ref.at[w], e_ref.at[w], r_ref.at[w], o_ref.at[w],
                da_ref, dqkvt_ref,
            )
        wsum_ref[3 * C :] += dot(o_ref[w].astype(BF16), grad_b)
        wsum_ref[: 3 * C] += dot(dqkvt_ref[...], nb_ref[w])
        d_normed = dot(w_ref[0], dqkvt_ref[...]).T
        normed = normed_ref[w]
        gsum_ref[...] += fold_tokens(d_normed * normed)
        out = grad + norm_back(d_normed, normed, inv_ref[w], gain_ref[0:1])
        out_ref[:, :, pl.ds(pl.multiple_of(w * WIN, WIN), WIN), :] = out.reshape(WIN, WIN, WIN, C)
        return carry

    lax.fori_loop(0, 4, window, 0)


def call(kernel, outs, scratch, *args, **params):
    whole = pl.BlockSpec(memory_space=pltpu.VMEM)
    return pl.pallas_call(
        kernel,
        out_shape=[jax.ShapeDtypeStruct(*o) for o in outs],
        in_specs=[whole] * len(args),
        out_specs=[whole] * len(outs),
        scratch_shapes=[pltpu.VMEM(*s) for s in scratch],
        compiler_params=pltpu.CompilerParams(vmem_limit_bytes=58 * 2**20, **params),
    )(*args)


def pass_along(value, axis, steps):
    count = lax.axis_size(axis)
    return lax.ppermute(value, axis, [(i, (i + steps) % count) for i in range(count)])


def pull_ahead(grid):
    ahead = jnp.concatenate([pass_along(grid[:, :, :32], "gy", -1), grid[:, :, 32:]], axis=2)
    return jnp.concatenate([ahead, pass_along(ahead[:1], "gx", -1)], axis=0)


def push_back(grid):
    back = jnp.concatenate([pass_along(grid[:, :, :32], "gy", 1), grid[:, :, 32:]], axis=2)
    return jnp.concatenate([pass_along(back[3:], "gx", 1), back], axis=0)


def local(tokens, cotangent, gains, qkv_weight, proj_weight):
    depth_count, row_count, col_count, features = tokens.shape
    total = depth_count * row_count * col_count * lax.axis_size("gy") * lax.axis_size("gx")
    factor = (total // 16) ** (-0.5)
    windows = col_count // WIN
    cot_win = (
        cotangent.reshape(WIN, WIN, windows, WIN, C).transpose(2, 0, 1, 3, 4).reshape(4, WIN, 64, C)
    )
    cot_ahead = pull_ahead(cot_win)
    weights = [((3 * C, C), BF16), ((C, 2 * C), BF16)]
    mid, e, r, o, qkvt, kv, nb, normed, inverse = call(
        kernel_forward,
        [
            ((4, WIN, 64, C), BF16),
            ((4, HEADS, TOK, TOK), BF16),
            ((4, 8, TOK), F32),
            ((4, C, TOK), F32),
            ((4, 3 * C, TOK), BF16),
            ((4, TOK, 2 * C), BF16),
            ((4, TOK, C), BF16),
            ((4, TOK, C), F32),
            ((4, TOK, 1), F32),
        ],
        [((WIN, WIN, 32, C), F32)] + weights + [((C, C), BF16)],
        tokens, gains, qkv_weight, proj_weight,
    )
    mid_ahead = pull_ahead(mid).reshape(5, TOK, C)
    grad, wsum_one, gsum_one = call(
        kernel_shifted,
        [((4, WIN, 64, C), BF16), ((4 * C, C), F32), ((8, C), F32)],
        [
            ((3 * C, TOK), BF16),
            ((TOK, 2 * C), BF16),
            ((C, TOK), BF16),
            ((C, TOK), F32),
            ((3 * C, TOK), BF16),
            ((2, HALF, HALF), F32),
        ]
        + weights,
        mid_ahead, cot_ahead.reshape(5, TOK, C), gains, qkv_weight, proj_weight,
    )
    grad_back = push_back(grad).reshape(5, TOK, C)
    out, wsum_zero, gsum_zero = call(
        kernel_backward,
        [((WIN, WIN, 32, C), F32), ((4 * C, C), F32), ((8, C), F32)],
        [((C, TOK), F32), ((3 * C, TOK), BF16)],
        grad_back, gains, qkv_weight, proj_weight, e, r, o, qkvt, kv, nb, normed, inverse,
    )
    wsum, gsum = lax.psum(
        (jnp.stack([wsum_zero, wsum_one]), jnp.stack([gsum_zero, gsum_one]).sum(1)), ("gy", "gx")
    )
    return (
        out,
        gsum * factor,
        wsum[:, : 3 * C].transpose(0, 2, 1) * factor,
        wsum[:, 3 * C :] * factor,
    )


def solution(mesh):
    in_specs = (P(None, "gy", "gx", None), P(None, "gy", "gx", None), P(), P(), P())
    out_specs = (P(None, "gy", "gx", None), P(), P(), P())
    return jax.shard_map(local, mesh=mesh, in_specs=in_specs, out_specs=out_specs, check_vma=False)
```

```python
import functools
import math

import jax
import jax.numpy as jnp
from jax import lax
from jax.experimental import pallas as pl
from jax.experimental.pallas import tpu as pltpu
from jax.sharding import PartitionSpec as P

HEADS = 6
WIN = 8
C = 192
HD = 32
TOK = WIN**3
HALF = TOK // 2
EPSILON = 1e-05
MASKED = -1e30
SCALE = HD**-0.5
LOG2E = 1.0 / math.log(2.0)
LN2 = math.log(2.0)
F32 = jnp.float32
BF16 = jnp.bfloat16
GROUPS = ((0, 1, 2), (3, 4, 5))


def dot(left, right):
    return jnp.dot(left, right, preferred_element_type=F32)


def dot_t(left, right):
    return lax.dot_general(left, right, (((1,), (1,)), ((), ())), preferred_element_type=F32)


def rows(head, part=0):
    start = part * C + head * HD
    return slice(start, start + HD)


def layer_norm(x, gain_row):
    center = x - jnp.sum(x, axis=-1, keepdims=True) * (1.0 / C)
    inverse = lax.rsqrt(jnp.sum(center * center, axis=-1, keepdims=True) * (1.0 / C) + EPSILON)
    normed = center * inverse
    return (normed * gain_row).astype(BF16), normed, inverse


def norm_back(d_normed, normed, inverse, gain_row):
    scaled = d_normed * gain_row
    first = jnp.sum(scaled, axis=-1, keepdims=True) * (1.0 / C)
    second = jnp.sum(scaled * normed, axis=-1, keepdims=True) * (1.0 / C)
    return inverse * (scaled - first - normed * second)


def fold_tokens(x):
    return jnp.sum(x.reshape(TOK // 8, 8, C), axis=0)


def halves(first, second):
    a = first.astype(F32).reshape(TOK // 8, 8, C)
    b = second.astype(F32).reshape(TOK // 8, 8, C)
    place = lax.broadcasted_iota(jnp.int32, (TOK // 8, 8, C), 1)
    return jnp.where(place < 4, a, b).reshape(TOK, C)


def prepare_weights(block, w_ref, p_ref, wt_ref, wkv_ref, pt_ref):
    weight = w_ref[block].astype(F32)
    wt_ref[...] = weight.T.astype(BF16)
    wkv_ref[...] = weight[:, C:].astype(BF16)
    if pt_ref is not None:
        pt_ref[...] = p_ref[block].astype(F32).T.astype(BF16)


def project(normed_b, wt_ref, wkv_ref, qkvt_ref, kv_ref):
    qkvt_ref[:C] = (dot_t(wt_ref[:C], normed_b) * (SCALE * LOG2E)).astype(BF16)
    qkvt_ref[C:] = dot_t(wt_ref[C:], normed_b).astype(BF16)
    kv_ref[...] = dot(normed_b, wkv_ref[...]).astype(BF16)


def regular_forward(group, qkvt_ref, kv_ref, e_ref, r_ref, o_ref):
    s = [dot(kv_ref[:, rows(h)], qkvt_ref[rows(h)]) for h in group]
    m = [jnp.max(x, axis=0, keepdims=True) for x in s]
    ef = [jnp.exp2(x - y) for x, y in zip(s, m)]
    e = [x.astype(BF16) for x in ef]
    for h, x in zip(group, e):
        e_ref[h] = x
    r = [1.0 / jnp.sum(x, axis=0, keepdims=True) for x in ef]
    o = [dot(qkvt_ref[rows(h, 2)], x) for h, x in zip(group, e)]
    for h, x, y in zip(group, o, r):
        o_ref[rows(h)] = x * y
        r_ref[h : h + 1] = y


def regular_backward(group, qkvt_ref, kv_ref, e_ref, r_ref, o_ref, da_ref, dqkvt_ref):
    da = [(da_ref[rows(h)] * r_ref[h : h + 1]).astype(BF16) for h in group]
    d = [
        jnp.sum(x.astype(F32) * o_ref[rows(h)], axis=0, keepdims=True) for h, x in zip(group, da)
    ]
    dp = [dot(kv_ref[:, rows(h, 1)], x) for h, x in zip(group, da)]
    for h, x in zip(group, da):
        dqkvt_ref[rows(h, 2)] = dot_t(x, e_ref[h]).astype(BF16)
    ds = [
        (e_ref[h].astype(F32) * (x - y)).astype(BF16) for h, x, y in zip(group, dp, d)
    ]
    for h, x in zip(group, ds):
        dqkvt_ref[rows(h)] = (dot(qkvt_ref[rows(h, 1)], x) * SCALE).astype(BF16)
        dqkvt_ref[rows(h, 1)] = (dot_t(qkvt_ref[rows(h)], x) * LN2).astype(BF16)


def shifted_both(group, qkvt_ref, kv_ref, bias, o_ref, da_ref, dqkvt_ref):
    parts = [(h, slice(k * HALF, (k + 1) * HALF)) for h in group for k in range(2)]
    s = [dot(kv_ref[t, rows(h)], qkvt_ref[rows(h), t]) + bias for h, t in parts]
    m = [jnp.max(x, axis=0, keepdims=True) for x in s]
    ef = [jnp.exp2(x - y) for x, y in zip(s, m)]
    e = [x.astype(BF16) for x in ef]
    r = [1.0 / jnp.sum(x, axis=0, keepdims=True) for x in ef]
    o = [dot(qkvt_ref[rows(h, 2), t], x) * y for (h, t), x, y in zip(parts, e, r)]
    da = [(da_ref[rows(h), t] * y).astype(BF16) for (h, t), y in zip(parts, r)]
    d = [jnp.sum(x.astype(F32) * y, axis=0, keepdims=True) for x, y in zip(da, o)]
    dp = [dot(kv_ref[t, rows(h, 1)], x) for (h, t), x in zip(parts, da)]
    for (h, t), x, y, z in zip(parts, o, da, e):
        o_ref[rows(h), t] = x.astype(BF16)
        dqkvt_ref[rows(h, 2), t] = dot_t(y, z).astype(BF16)
    ds = [(x.astype(F32) * (y - z)).astype(BF16) for x, y, z in zip(e, dp, d)]
    for (h, t), x in zip(parts, ds):
        dqkvt_ref[rows(h), t] = (dot(qkvt_ref[rows(h, 1), t], x) * SCALE).astype(BF16)
        dqkvt_ref[rows(h, 1), t] = (dot_t(qkvt_ref[rows(h), t], x) * LN2).astype(BF16)


def write_bias(bias_ref):
    last_row = lax.axis_index("gy") == lax.axis_size("gy") - 1
    last_col = lax.axis_index("gx") == lax.axis_size("gx") - 1
    key = lax.broadcasted_iota(jnp.int32, (HALF, HALF), 0)
    query = lax.broadcasted_iota(jnp.int32, (HALF, HALF), 1)
    row_bias = jnp.where((key // 32) % 2 != (query // 32) % 2, MASKED, 0.0).astype(F32)
    col_bias = jnp.where((key // 4) % 2 != (query // 4) % 2, MASKED, 0.0).astype(F32)
    row_bias = row_bias * jnp.where(last_row, 1.0, 0.0).astype(F32)
    col_bias = col_bias * jnp.where(last_col, 1.0, 0.0).astype(F32)
    bias_ref[0] = row_bias
    bias_ref[1] = jnp.minimum(row_bias, col_bias)


def remote(src, dst, send, recv, target):
    return pltpu.make_async_remote_copy(
        src_ref=src,
        dst_ref=dst,
        send_sem=send,
        recv_sem=recv,
        device_id=target,
        device_id_type=pl.DeviceIdType.MESH,
    )


def loop(first, last, body):
    def step(i, carry):
        body(i)
        return carry

    lax.fori_loop(first, last, step, 0)


class Place:
    def __init__(self):
        self.ny, self.nx = lax.axis_size("gy"), lax.axis_size("gx")
        self.y, self.x = lax.axis_index("gy"), lax.axis_index("gx")

    def at(self, dy, dx):
        return (lax.rem(self.y + dy + self.ny, self.ny), lax.rem(self.x + dx + self.nx, self.nx))


def greet(place):
    barrier = pltpu.get_barrier_semaphore()

    def signal(target):
        pl.semaphore_signal(barrier, 1, device_id=target, device_id_type=pl.DeviceIdType.MESH)

    loop(1, place.ny, lambda i: signal(place.at(i, 0)))
    loop(1, place.nx, lambda i: signal(place.at(0, i)))
    signal(place.at(1, 1))
    signal(place.at(-1, -1))
    pl.semaphore_wait(barrier, place.ny + place.nx)


class Halo:
    def __init__(self, place, step, own, grid, send, recv):
        self.place, self.step, self.own, self.grid = place, step, own, grid
        self.send, self.recv = send, recv
        self.edge, self.into, self.base = (0, 4, 0) if step < 0 else (3, 0, 1)

    def row(self, w):
        return remote(
            self.own.at[w, :, 0:32],
            self.grid.at[w + self.base, :, 0:32],
            self.send.at[w],
            self.recv.at[w],
            self.place.at(self.step, 0),
        )

    def column(self):
        return remote(
            self.own.at[self.edge, :, 32:64],
            self.grid.at[self.into, :, 32:64],
            self.send.at[4],
            self.recv.at[4],
            self.place.at(0, self.step),
        )

    def corner(self):
        return remote(
            self.own.at[self.edge, :, 0:32],
            self.grid.at[self.into, :, 0:32],
            self.send.at[5],
            self.recv.at[5],
            self.place.at(self.step, self.step),
        )

    def start(self, w, values):
        self.own[w] = values
        self.grid[w + self.base, :, 32:64] = values[:, 32:64]
        self.row(w).start()

        @pl.when(w == self.edge)
        def _():
            self.column().start()
            self.corner().start()

    def arrived(self, w):
        self.row(w).wait_recv()

    def edge_arrived(self):
        self.column().wait_recv()
        self.corner().wait_recv()

    def finish(self):
        loop(0, 4, lambda w: self.row(w).wait_send())
        self.column().wait_send()
        self.corner().wait_send()


class Reduce:
    def __init__(self, place, total, chunks, part, mid, full, sems):
        self.place, self.total, self.chunks = place, total, chunks
        self.part, self.mid, self.full = part, mid, full
        self.s1, self.r1, self.s2, self.r2, self.s3, self.r3 = sems

    def scatter(self, i):
        to = self.place.at(i, 0)
        return remote(
            self.chunks.at[to[0]], self.part.at[i - 1], self.s1.at[i - 1], self.r1.at[i - 1], to
        )

    def across(self, i):
        mine = self.mid.at[self.place.x]
        return remote(mine, mine, self.s2.at[i - 1], self.r2.at[self.place.x], self.place.at(0, i))

    def gather(self, i):
        mine = self.full.at[self.place.y]
        return remote(mine, mine, self.s3.at[i - 1], self.r3.at[self.place.y], self.place.at(i, 0))

    def start(self, gsum):
        gain = jnp.sum(gsum, axis=0, keepdims=True)
        first = lax.broadcasted_iota(jnp.int32, (8, 64), 0) == 0
        self.total[:, C:] = jnp.zeros((self.total.shape[0], 64), F32)
        for k in range(3):
            piece = jnp.broadcast_to(gain[:, 64 * k : 64 * k + 64], (8, 64))
            self.total[8 * k : 8 * k + 8, C:] = jnp.where(first, piece, 0.0)
        self.chunks[...] = self.total[...].astype(BF16).reshape(self.chunks.shape)
        loop(1, self.place.ny, lambda i: self.scatter(i).start())

    def middle(self):
        loop(1, self.place.ny, lambda i: self.scatter(i).wait_recv())
        size = self.chunks.shape[1]
        acc = self.total[pl.ds(pl.multiple_of(self.place.y * size, 16), size)]
        for i in range(self.place.ny - 1):
            acc += self.part[i].astype(F32)
        self.mid[self.place.x] = acc.astype(BF16)
        loop(1, self.place.nx, lambda i: self.across(i).start())

    def spread(self, factor):
        def arrived(i):
            x = self.place.at(0, i)[1]
            remote(
                self.mid.at[x], self.mid.at[x], self.s2.at[i - 1], self.r2.at[x], self.place.at(0, i)
            ).wait_recv()

        loop(1, self.place.nx, arrived)
        acc = self.mid[0].astype(F32)
        for i in range(1, self.place.nx):
            acc += self.mid[i].astype(F32)
        self.full[self.place.y] = (acc * factor).astype(BF16)
        loop(1, self.place.ny, lambda i: self.gather(i).start())

    def finish(self, block, gain_ref, qkv_ref, proj_ref):
        def arrived(i):
            y = self.place.at(i, 0)[0]
            remote(
                self.full.at[y], self.full.at[y], self.s3.at[i - 1], self.r3.at[y], self.place.at(i, 0)
            ).wait_recv()

        loop(1, self.place.ny, arrived)
        whole = self.full[...].reshape(self.total.shape).astype(F32)
        qkv_ref[block] = whole[: 3 * C, :C].T
        proj_ref[block] = whole[3 * C :, :C]
        for k in range(3):
            gain_ref[block : block + 1, 64 * k : 64 * k + 64] = whole[8 * k : 8 * k + 1, C:]

    def drain(self):
        loop(1, self.place.ny, lambda i: self.scatter(i).wait_send())
        loop(1, self.place.nx, lambda i: self.across(i).wait_send())
        loop(1, self.place.ny, lambda i: self.gather(i).wait_send())


def kernel(
    factor,
    tok_ref, cot_ref, gain_ref, w_ref, p_ref,
    out_ref, ggain_ref, gqkv_ref, gproj_ref,
    x32_ref, wt_ref, wkv_ref, pt_ref, bias_ref,
    e_ref, r_ref, o_ref, qkvt_ref, kv_ref, nb_ref, normed_ref, inv_ref,
    qkvt1_ref, kv1_ref, o1_ref, da_ref, dqkvt_ref, total_ref, gsum_ref,
    own_ref, grid_ref, chunks_ref, part_ref, mid_ref, full_ref,
    hsend, hrecv, s1, r1, s2, r2, s3, r3,
):
    place = Place()
    greet(place)
    cot, middle, back = (
        Halo(place, step, own_ref.at[k], grid_ref.at[k], hsend.at[k], hrecv.at[k])
        for k, step in enumerate((-1, -1, 1))
    )
    sums = [
        Reduce(
            place, total_ref.at[k], chunks_ref.at[k], part_ref.at[k], mid_ref.at[k], full_ref.at[k],
            [s.at[k] for s in (s1, r1, s2, r2, s3, r3)],
        )
        for k in range(2)
    ]

    def columns(w):
        return pl.ds(pl.multiple_of(w * WIN, WIN), WIN)

    x32_ref[...] = cot_ref[...].astype(F32)

    def send_cotangent(w):
        cot.start(w, x32_ref[:, :, columns(w), :].reshape(TOK, C).astype(BF16).reshape(WIN, 64, C))

    loop(0, 4, send_cotangent)

    x32_ref[...] = tok_ref[...].astype(F32)
    for block in range(2):
        prepare_weights(
            block, w_ref, p_ref, wt_ref.at[block], wkv_ref.at[block], None if block else pt_ref
        )
    write_bias(bias_ref)
    total_ref[...] = jnp.zeros_like(total_ref)
    gsum_ref[...] = jnp.zeros_like(gsum_ref)

    def regular_window(w):
        x = x32_ref[:, :, columns(w), :].reshape(TOK, C)
        normed_b, normed, inverse = layer_norm(x, gain_ref[0:1])
        nb_ref[w] = normed_b
        normed_ref[w] = normed
        inv_ref[w] = inverse
        project(normed_b, wt_ref.at[0], wkv_ref.at[0], qkvt_ref.at[w], kv_ref.at[w])
        for group in GROUPS:
            regular_forward(
                group, qkvt_ref.at[w], kv_ref.at[w], e_ref.at[w], r_ref.at[w], o_ref.at[w]
            )
        branch = dot(pt_ref[...], o_ref[w].astype(BF16)).T
        middle.start(w, (x + branch).astype(BF16).reshape(WIN, 64, C))

    loop(0, 4, regular_window)

    loop(0, 4, cot.arrived)
    cot.edge_arrived()
    middle.arrived(0)

    def shifted_window(w):
        @pl.when(w < 3)
        def _():
            middle.arrived(w + 1)

        @pl.when(w == 3)
        def _():
            middle.edge_arrived()

        x = halves(middle.grid[w + 1].reshape(TOK, C), middle.grid[w].reshape(TOK, C))
        normed_b, normed, inverse = layer_norm(x, gain_ref[1:2])
        project(normed_b, wt_ref.at[1], wkv_ref.at[1], qkvt1_ref, kv1_ref)
        g = halves(cot.grid[w + 1].reshape(TOK, C), cot.grid[w].reshape(TOK, C))
        g_b = g.astype(BF16)
        da_ref[...] = dot_t(p_ref[1], g_b)
        bias = bias_ref[w // 3]
        for group in GROUPS:
            shifted_both(group, qkvt1_ref, kv1_ref, bias, o1_ref, da_ref, dqkvt_ref)
        total_ref[1, 3 * C :, :C] += dot(o1_ref[...], g_b)
        total_ref[1, : 3 * C, :C] += dot(dqkvt_ref[...], normed_b)
        d_normed = dot(w_ref[1], dqkvt_ref[...]).T
        gsum_ref[1] += fold_tokens(d_normed * normed)
        grad = g + norm_back(d_normed, normed, inverse, gain_ref[1:2])
        back.start(w, grad.astype(BF16).reshape(WIN, 64, C))

    loop(0, 4, shifted_window)
    sums[1].start(gsum_ref[1])
    back.arrived(0)

    def backward_window(t):
        w = lax.rem(t + 1, 4)

        @pl.when(t < 3)
        def _():
            back.arrived(t + 1)

        @pl.when(t == 3)
        def _():
            back.edge_arrived()

        @pl.when(t == 1)
        def _():
            sums[1].middle()

        @pl.when(t == 2)
        def _():
            sums[1].spread(factor)

        g = halves(back.grid[w].reshape(TOK, C), back.grid[w + 1].reshape(TOK, C))
        g_b = g.astype(BF16)
        da_ref[...] = dot_t(p_ref[0], g_b)
        for group in GROUPS:
            regular_backward(
                group, qkvt_ref.at[w], kv_ref.at[w], e_ref.at[w], r_ref.at[w], o_ref.at[w],
                da_ref, dqkvt_ref,
            )
        total_ref[0, 3 * C :, :C] += dot(o_ref[w].astype(BF16), g_b)
        total_ref[0, : 3 * C, :C] += dot(dqkvt_ref[...], nb_ref[w])
        d_normed = dot(w_ref[0], dqkvt_ref[...]).T
        normed = normed_ref[w]
        gsum_ref[0] += fold_tokens(d_normed * normed)
        out = g + norm_back(d_normed, normed, inv_ref[w], gain_ref[0:1])
        out_ref[:, :, columns(w), :] = out.reshape(WIN, WIN, WIN, C)

    loop(0, 4, backward_window)
    sums[0].start(gsum_ref[0])
    sums[1].finish(1, ggain_ref, gqkv_ref, gproj_ref)
    sums[0].middle()
    for halo in (cot, middle, back):
        halo.finish()
    sums[1].drain()
    sums[0].spread(factor)
    sums[0].finish(0, ggain_ref, gqkv_ref, gproj_ref)
    sums[0].drain()


def local(tokens, cotangent, gains, qkv_weight, proj_weight):
    depth_count, row_count, col_count, features = tokens.shape
    ny, nx = lax.axis_size("gy"), lax.axis_size("gx")
    factor = (depth_count * row_count * col_count * ny * nx // 16) ** (-0.5)
    size = 4 * C // ny
    whole = pl.BlockSpec(memory_space=pltpu.VMEM)
    outs = [((WIN, WIN, 32, C), F32), ((2, C), F32), ((2, C, 3 * C), F32), ((2, C, C), F32)]
    scratch = [
        ((WIN, WIN, 32, C), F32),
        ((2, 3 * C, C), BF16),
        ((2, C, 2 * C), BF16),
        ((C, C), BF16),
        ((2, HALF, HALF), F32),
        ((4, HEADS, TOK, TOK), BF16),
        ((4, 8, TOK), F32),
        ((4, C, TOK), F32),
        ((4, 3 * C, TOK), BF16),
        ((4, TOK, 2 * C), BF16),
        ((4, TOK, C), BF16),
        ((4, TOK, C), F32),
        ((4, TOK, 1), F32),
        ((3 * C, TOK), BF16),
        ((TOK, 2 * C), BF16),
        ((C, TOK), BF16),
        ((C, TOK), F32),
        ((3 * C, TOK), BF16),
        ((2, 4 * C, 256), F32),
        ((2, 8, C), F32),
        ((3, 4, WIN, 64, C), BF16),
        ((3, 5, WIN, 64, C), BF16),
        ((2, ny, size, 256), BF16),
        ((2, ny - 1, size, 256), BF16),
        ((2, nx, size, 256), BF16),
        ((2, ny, size, 256), BF16),
    ]
    sems = [(3, 6), (3, 6), (2, ny), (2, ny), (2, nx), (2, nx), (2, ny), (2, ny)]
    return pl.pallas_call(
        functools.partial(kernel, factor),
        out_shape=[jax.ShapeDtypeStruct(*o) for o in outs],
        in_specs=[whole] * 5,
        out_specs=[whole] * 4,
        scratch_shapes=[pltpu.VMEM(*s) for s in scratch]
        + [pltpu.SemaphoreType.DMA(s) for s in sems],
        compiler_params=pltpu.CompilerParams(
            vmem_limit_bytes=60 * 2**20, collective_id=0, has_side_effects=True
        ),
    )(tokens, cotangent, gains, qkv_weight, proj_weight)


def solution(mesh):
    in_specs = (P(None, "gy", "gx", None), P(None, "gy", "gx", None), P(), P(), P())
    out_specs = (P(None, "gy", "gx", None), P(), P(), P())
    return jax.shard_map(local, mesh=mesh, in_specs=in_specs, out_specs=out_specs, check_vma=False)
```

```python
import functools
import math

import jax
import jax.numpy as jnp
from jax import lax
from jax.experimental import pallas as pl
from jax.experimental.pallas import tpu as pltpu
from jax.sharding import PartitionSpec as P

HEADS = 6
WIN = 8
C = 192
HD = 32
TOK = WIN**3
HALF = TOK // 2
EPSILON = 1e-05
MASKED = -1e30
SCALE = HD**-0.5
LOG2E = 1.0 / math.log(2.0)
LN2 = math.log(2.0)
F32 = jnp.float32
BF16 = jnp.bfloat16
GROUPS = ((0, 1, 2), (3, 4, 5))
FIRST = 384
PIECES = ((0, 512), (512, 768))


def dot(left, right):
    return jnp.dot(left, right, preferred_element_type=F32)


def dot_t(left, right):
    return lax.dot_general(left, right, (((1,), (1,)), ((), ())), preferred_element_type=F32)


def rows(head, part=0):
    start = part * 128 + head * HD if head < 4 else FIRST + part * 64 + (head - 4) * HD
    return slice(start, start + HD)


def own_rows(head):
    return slice(head * HD, head * HD + HD)


def columns_of(head, part):
    start = part * 128 + head * HD if head < 4 else 256 + part * 64 + (head - 4) * HD
    return slice(start, start + HD)


def layer_norm(x, gain_row):
    center = x - jnp.sum(x, axis=-1, keepdims=True) * (1.0 / C)
    inverse = lax.rsqrt(jnp.sum(center * center, axis=-1, keepdims=True) * (1.0 / C) + EPSILON)
    normed = center * inverse
    return (normed * gain_row).astype(BF16), normed, inverse


def norm_back(d_normed, normed, inverse, gain_row):
    scaled = d_normed * gain_row
    first = jnp.sum(scaled, axis=-1, keepdims=True) * (1.0 / C)
    second = jnp.sum(scaled * normed, axis=-1, keepdims=True) * (1.0 / C)
    return inverse * (scaled - first - normed * second)


def halves(first, second):
    a = first.astype(F32).reshape(TOK // 8, 8, C)
    b = second.astype(F32).reshape(TOK // 8, 8, C)
    place = lax.broadcasted_iota(jnp.int32, (TOK // 8, 8, C), 1)
    return jnp.where(place < 4, a, b).reshape(TOK, C)


def prepare_weights(block, w_ref, p_ref, wt_ref, wp_ref, wkv_ref, pt_ref):
    turned = w_ref[block].astype(F32).T
    starts = ((0, 128), (C, C + 128), (2 * C, 2 * C + 128), (128, C), (C + 128, 2 * C), (2 * C + 128, 3 * C))
    turned = jnp.concatenate([turned[a:b] for a, b in starts], axis=0)
    wt_ref[...] = turned.astype(BF16)
    wp_ref[...] = turned.T.astype(BF16)
    wkv_ref[...] = jnp.concatenate([turned[128:FIRST], turned[FIRST + 64 :]], axis=0).T.astype(BF16)
    if pt_ref is not None:
        pt_ref[...] = p_ref[block].astype(F32).T.astype(BF16)


def project(normed_b, wt_ref, wkv_ref, qkvt_ref, kv_ref):
    qkvt = dot_t(wt_ref[...], normed_b)
    qkvt_ref[:128] = (qkvt[:128] * (SCALE * LOG2E)).astype(BF16)
    qkvt_ref[128:FIRST] = qkvt[128:FIRST].astype(BF16)
    qkvt_ref[FIRST : FIRST + 64] = (qkvt[FIRST : FIRST + 64] * (SCALE * LOG2E)).astype(BF16)
    qkvt_ref[FIRST + 64 :] = qkvt[FIRST + 64 :].astype(BF16)
    kv_ref[...] = dot(normed_b, wkv_ref[...]).astype(BF16)


def regular_forward(group, qkvt_ref, kv_ref, e_ref, r_ref, o_ref):
    s = [dot(kv_ref[:, columns_of(h, 0)], qkvt_ref[rows(h)]) for h in group]
    m = [jnp.max(x, axis=0, keepdims=True) for x in s]
    ef = [jnp.exp2(x - y) for x, y in zip(s, m)]
    e = [x.astype(BF16) for x in ef]
    for h, x in zip(group, e):
        e_ref[h] = x
    r = [1.0 / jnp.sum(x, axis=0, keepdims=True) for x in ef]
    o = [dot(qkvt_ref[rows(h, 2)], x) for h, x in zip(group, e)]
    for h, x, y in zip(group, o, r):
        o_ref[own_rows(h)] = x * y
        r_ref[h : h + 1] = y


def regular_backward(group, qkvt_ref, kv_ref, e_ref, r_ref, o_ref, da_ref, dqkvt_ref):
    da = [(da_ref[own_rows(h)] * r_ref[h : h + 1]).astype(BF16) for h in group]
    d = [
        jnp.sum(x.astype(F32) * o_ref[own_rows(h)], axis=0, keepdims=True) for h, x in zip(group, da)
    ]
    dp = [dot(kv_ref[:, columns_of(h, 1)], x) for h, x in zip(group, da)]
    for h, x in zip(group, da):
        dqkvt_ref[rows(h, 2)] = dot_t(x, e_ref[h]).astype(BF16)
    ds = [
        (e_ref[h].astype(F32) * (x - y)).astype(BF16) for h, x, y in zip(group, dp, d)
    ]
    for h, x in zip(group, ds):
        dqkvt_ref[rows(h)] = (dot(qkvt_ref[rows(h, 1)], x) * SCALE).astype(BF16)
        dqkvt_ref[rows(h, 1)] = (dot_t(qkvt_ref[rows(h)], x) * LN2).astype(BF16)


def shifted_both(group, qkvt_ref, kv_ref, bias, o_ref, da_ref, dqkvt_ref):
    parts = [(h, slice(k * HALF, (k + 1) * HALF)) for h in group for k in range(2)]
    s = [dot(kv_ref[t, columns_of(h, 0)], qkvt_ref[rows(h), t]) + bias for h, t in parts]
    m = [jnp.max(x, axis=0, keepdims=True) for x in s]
    ef = [jnp.exp2(x - y) for x, y in zip(s, m)]
    e = [x.astype(BF16) for x in ef]
    r = [1.0 / jnp.sum(x, axis=0, keepdims=True) for x in ef]
    o = [dot(qkvt_ref[rows(h, 2), t], x) * y for (h, t), x, y in zip(parts, e, r)]
    da = [(da_ref[own_rows(h), t] * y).astype(BF16) for (h, t), y in zip(parts, r)]
    d = [jnp.sum(x.astype(F32) * y, axis=0, keepdims=True) for x, y in zip(da, o)]
    dp = [dot(kv_ref[t, columns_of(h, 1)], x) for (h, t), x in zip(parts, da)]
    for (h, t), x, y, z in zip(parts, o, da, e):
        o_ref[own_rows(h), t] = x.astype(BF16)
        dqkvt_ref[rows(h, 2), t] = dot_t(y, z).astype(BF16)
    ds = [(x.astype(F32) * (y - z)).astype(BF16) for x, y, z in zip(e, dp, d)]
    for (h, t), x in zip(parts, ds):
        dqkvt_ref[rows(h), t] = (dot(qkvt_ref[rows(h, 1), t], x) * SCALE).astype(BF16)
        dqkvt_ref[rows(h, 1), t] = (dot_t(qkvt_ref[rows(h), t], x) * LN2).astype(BF16)


def write_bias(bias_ref):
    last_row = lax.axis_index("gy") == lax.axis_size("gy") - 1
    last_col = lax.axis_index("gx") == lax.axis_size("gx") - 1
    key = lax.broadcasted_iota(jnp.int32, (HALF, HALF), 0)
    query = lax.broadcasted_iota(jnp.int32, (HALF, HALF), 1)
    row_bias = jnp.where((key // 32) % 2 != (query // 32) % 2, MASKED, 0.0).astype(F32)
    col_bias = jnp.where((key // 4) % 2 != (query // 4) % 2, MASKED, 0.0).astype(F32)
    row_bias = row_bias * jnp.where(last_row, 1.0, 0.0).astype(F32)
    col_bias = col_bias * jnp.where(last_col, 1.0, 0.0).astype(F32)
    bias_ref[0] = row_bias
    bias_ref[1] = jnp.minimum(row_bias, col_bias)


def remote(src, dst, send, recv, target):
    return pltpu.make_async_remote_copy(
        src_ref=src,
        dst_ref=dst,
        send_sem=send,
        recv_sem=recv,
        device_id=target,
        device_id_type=pl.DeviceIdType.MESH,
    )


def loop(first, last, body):
    def step(i, carry):
        body(i)
        return carry

    lax.fori_loop(first, last, step, 0)


def sizes_of(ny, nx):
    along_x = min(4, ny // 2)
    return along_x, ny // (2 * along_x), nx // 2


class Place:
    def __init__(self):
        self.ny, self.nx = lax.axis_size("gy"), lax.axis_size("gx")
        self.y, self.x = lax.axis_index("gy"), lax.axis_index("gx")
        self.nxx, self.nlow, self.nz = sizes_of(self.ny, self.nx)
        self.n1, self.n2 = self.nxx * self.nz, 4 * self.nlow
        core, across = lax.rem(self.y, 2), lax.rem(self.y // 2, self.nxx)
        low, z, high = self.y // (2 * self.nxx), self.x // 2, lax.rem(self.x, 2)
        self.core, self.low, self.high = core, low, high
        self.plane = across * self.nz + z
        self.across, self.z = across, z
        self.stack = (core * self.nlow + low) * 2 + high

    def at(self, dy, dx):
        return (lax.rem(self.y + dy + self.ny, self.ny), lax.rem(self.x + dx + self.nx, self.nx))

    def in_plane(self, i):
        k = lax.rem(self.plane + i, self.n1)
        across, z = k // self.nz, lax.rem(k, self.nz)
        return (self.low * (2 * self.nxx) + across * 2 + self.core, z * 2 + self.high), k

    def in_stack(self, i):
        k = lax.rem(self.stack + i, self.n2)
        core, low, high = k // (2 * self.nlow), lax.rem(k // 2, self.nlow), lax.rem(k, 2)
        return (low * (2 * self.nxx) + self.across * 2 + core, self.z * 2 + high), k


def greet(place):
    barrier = pltpu.get_barrier_semaphore()

    def signal(target):
        pl.semaphore_signal(barrier, 1, device_id=target, device_id_type=pl.DeviceIdType.MESH)

    loop(1, place.n1, lambda i: signal(place.in_plane(i)[0]))
    loop(1, place.n2, lambda i: signal(place.in_stack(i)[0]))
    for step in (-1, 1):
        signal(place.at(step, 0))
        signal(place.at(0, step))
        signal(place.at(step, step))
    return lambda: pl.semaphore_wait(barrier, place.n1 + place.n2 + 4)


def pack(window):
    pairs = window.astype(F32).reshape(32, 2, 8, C)
    place = lax.broadcasted_iota(jnp.int32, (32, 8, C), 1)
    packed = jnp.where(place < 4, pairs[:, 0], pltpu.roll(pairs[:, 1], 4, 1))
    return packed.astype(BF16).reshape(8, 32, C)


def unpack(packed):
    values = packed.astype(F32).reshape(32, 8, C)
    pairs = jnp.stack([values, pltpu.roll(values, 4, 1)], axis=1)
    return pairs.reshape(TOK, C).astype(BF16).reshape(8, 64, C)


class Halo:
    def __init__(self, place, step, own, grid, edge_own, edge_grid, send, recv):
        self.place, self.step, self.own, self.grid = place, step, own, grid
        self.edge_own, self.edge_grid = edge_own, edge_grid
        self.send, self.recv = send, recv
        self.edge, self.into, self.base = (0, 4, 0) if step < 0 else (3, 0, 1)

    def row(self, w):
        return remote(
            self.own.at[w, :, 0:32],
            self.grid.at[w + self.base, :, 0:32],
            self.send.at[w],
            self.recv.at[w],
            self.place.at(self.step, 0),
        )

    def column(self):
        return remote(
            self.edge_own.at[:, 16:32],
            self.edge_grid.at[:, 16:32],
            self.send.at[4],
            self.recv.at[4],
            self.place.at(0, self.step),
        )

    def corner(self):
        return remote(
            self.edge_own.at[:, 0:16],
            self.edge_grid.at[:, 0:16],
            self.send.at[5],
            self.recv.at[5],
            self.place.at(self.step, self.step),
        )

    def stage(self, w, values):
        self.own[w] = values
        self.grid[w + self.base, :, 32:64] = values[:, 32:64]

        @pl.when(w == self.edge)
        def _():
            self.edge_own[...] = pack(values)

    def start(self, w):
        self.row(w).start()

        @pl.when(w == self.edge)
        def _():
            self.column().start()
            self.corner().start()

    def arrived(self, w):
        self.row(w).wait_recv()

    def edge_arrived(self):
        self.column().wait_recv()
        self.corner().wait_recv()
        self.grid[self.into] = unpack(self.edge_grid[...])

    def finish(self):
        loop(0, 4, lambda w: self.row(w).wait_send())
        self.column().wait_send()
        self.corner().wait_send()


class Reduce:
    def __init__(self, place, total, chunks, part, mid, full, sems):
        self.place, self.total, self.chunks = place, total, chunks
        self.part, self.mid, self.full = part, mid, full
        self.s1, self.r1, self.s2, self.r2, self.s3, self.r3 = sems

    def scatter(self, i):
        to, k = self.place.in_plane(i)
        return remote(self.chunks.at[k], self.part.at[i - 1], self.s1.at[i - 1], self.r1.at[i - 1], to)

    def across(self, i):
        mine = self.mid.at[self.place.stack]
        to = self.place.in_stack(i)[0]
        return remote(mine, mine, self.s2.at[i - 1], self.r2.at[self.place.stack], to)

    def gather(self, i):
        mine = self.full.at[self.place.plane]
        to = self.place.in_plane(i)[0]
        return remote(mine, mine, self.s3.at[i - 1], self.r3.at[self.place.plane], to)

    def start(self):
        self.chunks[...] = self.total[...].astype(BF16).reshape(self.chunks.shape)
        loop(1, self.place.n1, lambda i: self.scatter(i).start())

    def middle(self):
        loop(1, self.place.n1, lambda i: self.scatter(i).wait_recv())
        size = self.chunks.shape[1]
        acc = self.total[pl.ds(pl.multiple_of(self.place.plane * size, 16), size)]
        for i in range(self.place.n1 - 1):
            acc += self.part[i].astype(F32)
        self.mid[self.place.stack] = acc.astype(BF16)
        loop(1, self.place.n2, lambda i: self.across(i).start())

    def spread(self, factor):
        def arrived(i):
            to, k = self.place.in_stack(i)
            remote(self.mid.at[k], self.mid.at[k], self.s2.at[i - 1], self.r2.at[k], to).wait_recv()

        loop(1, self.place.n2, arrived)
        acc = self.mid[0].astype(F32)
        for i in range(1, self.place.n2):
            acc += self.mid[i].astype(F32)
        self.full[self.place.plane] = (acc * factor).astype(BF16)
        loop(1, self.place.n1, lambda i: self.gather(i).start())

    def finish(self, result):
        def arrived(i):
            to, k = self.place.in_plane(i)
            remote(self.full.at[k], self.full.at[k], self.s3.at[i - 1], self.r3.at[k], to).wait_recv()

        loop(1, self.place.n1, arrived)
        result[...] = self.full[...].reshape(result.shape)

    def drain(self):
        loop(1, self.place.n1, lambda i: self.scatter(i).wait_send())
        loop(1, self.place.n2, lambda i: self.across(i).wait_send())
        loop(1, self.place.n1, lambda i: self.gather(i).wait_send())


def kernel(
    factor,
    tok_ref, cot_ref, gain_ref, w_ref, p_ref,
    out_ref, res1_ref, resa_ref, resb_ref,
    x32_ref, wt_ref, wp_ref, wkv_ref, pt_ref, bias_ref,
    e_ref, r_ref, o_ref, qkvt_ref, kv_ref, nb_ref, normed_ref, inv_ref,
    qkvt1_ref, kv1_ref, o1_ref, da_ref, dqkvt_ref, gb_ref, total_ref,
    own_ref, grid_ref, edge_own_ref, edge_grid_ref,
    ch1, pa1, mi1, fu1, cha, paa, mia, fua, chb, pab, mib, fub,
    hsend, hrecv, s1, r1, s2, r2, s3, r3, osem,
):
    place = Place()
    wait_for_peers = greet(place)
    cot, middle, back = (
        Halo(
            place, step, own_ref.at[k], grid_ref.at[k], edge_own_ref.at[k], edge_grid_ref.at[k],
            hsend.at[k], hrecv.at[k],
        )
        for k, step in enumerate((-1, -1, 1))
    )
    sum1, suma, sumb = (
        Reduce(place, total, *refs, [s.at[k] for s in (s1, r1, s2, r2, s3, r3)])
        for k, (total, refs) in enumerate(
            [
                (total_ref.at[1], (ch1, pa1, mi1, fu1)),
                (total_ref.at[0, slice(*PIECES[0])], (cha, paa, mia, fua)),
                (total_ref.at[0, slice(*PIECES[1])], (chb, pab, mib, fub)),
            ]
        )
    )

    def columns(w):
        return pl.ds(pl.multiple_of(w * WIN, WIN), WIN)

    x32_ref[...] = cot_ref[...].astype(F32)

    def stage_cotangent(w):
        cot.stage(w, x32_ref[:, :, columns(w), :].reshape(TOK, C).astype(BF16).reshape(WIN, 64, C))

    loop(0, 4, stage_cotangent)

    x32_ref[...] = tok_ref[...].astype(F32)
    for block in range(2):
        prepare_weights(
            block, w_ref, p_ref, wt_ref.at[block], wp_ref.at[block], wkv_ref.at[block],
            None if block else pt_ref,
        )
    write_bias(bias_ref)
    total_ref[...] = jnp.zeros_like(total_ref)

    def regular_window(w):
        x = x32_ref[:, :, columns(w), :].reshape(TOK, C)
        normed_b, normed, inverse = layer_norm(x, gain_ref[0:1])
        nb_ref[w] = normed_b
        normed_ref[w] = normed
        inv_ref[w] = inverse
        project(normed_b, wt_ref.at[0], wkv_ref.at[0], qkvt_ref.at[w], kv_ref.at[w])
        for group in GROUPS:
            regular_forward(
                group, qkvt_ref.at[w], kv_ref.at[w], e_ref.at[w], r_ref.at[w], o_ref.at[w]
            )
        branch = dot(pt_ref[...], o_ref[w].astype(BF16)).T
        middle.stage(w, (x + branch).astype(BF16).reshape(WIN, 64, C))

        @pl.when(w == 0)
        def _():
            wait_for_peers()
            loop(0, 4, cot.start)

        middle.start(w)

    loop(0, 4, regular_window)

    loop(0, 4, cot.arrived)
    cot.edge_arrived()
    middle.arrived(0)

    def shifted_window(w):
        @pl.when(w < 3)
        def _():
            middle.arrived(w + 1)

        @pl.when(w == 3)
        def _():
            middle.edge_arrived()

        x = halves(middle.grid[w + 1].reshape(TOK, C), middle.grid[w].reshape(TOK, C))
        normed_b, normed, inverse = layer_norm(x, gain_ref[1:2])
        project(normed_b, wt_ref.at[1], wkv_ref.at[1], qkvt1_ref, kv1_ref)
        g = halves(cot.grid[w + 1].reshape(TOK, C), cot.grid[w].reshape(TOK, C))
        g_b = g.astype(BF16)
        da_ref[0] = dot_t(p_ref[1], g_b)
        bias = bias_ref[w // 3]
        for group in GROUPS:
            shifted_both(group, qkvt1_ref, kv1_ref, bias, o1_ref, da_ref.at[0], dqkvt_ref.at[0])
        add_projection(total_ref.at[1], o1_ref[...], g_b)
        sums = dot(dqkvt_ref[0], normed_b)
        total_ref[1, :FIRST] += sums[:FIRST]
        total_ref[1, 512:704] += sums[FIRST:]
        d_normed = dot(wp_ref[1], dqkvt_ref[0]).T
        grad = g + norm_back(d_normed, normed, inverse, gain_ref[1:2])
        back.stage(w, grad.astype(BF16).reshape(WIN, 64, C))
        back.start(w)

    loop(0, 4, shifted_window)
    sum1.start()
    back.arrived(0)

    def first_heads(t):
        w = lax.rem(t + 1, 4)

        @pl.when(t < 3)
        def _():
            back.arrived(t + 1)

        @pl.when(t == 3)
        def _():
            back.edge_arrived()

        @pl.when(t == 3)
        def _():
            sum1.middle()

        g = halves(back.grid[w].reshape(TOK, C), back.grid[w + 1].reshape(TOK, C))
        g_b = g.astype(BF16)
        gb_ref[w] = g_b
        da_ref[w] = dot_t(p_ref[0], g_b)
        for group in ((0, 1), (2, 3)):
            regular_backward(
                group, qkvt_ref.at[w], kv_ref.at[w], e_ref.at[w], r_ref.at[w], o_ref.at[w],
                da_ref.at[w], dqkvt_ref.at[w],
            )
        add_projection(total_ref.at[0], o_ref[w].astype(BF16), g_b)
        total_ref[0, :FIRST] += dot(dqkvt_ref[w, :FIRST], nb_ref[w])

    loop(0, 4, first_heads)
    suma.start()

    def last_heads(w):
        @pl.when(w == 2)
        def _():
            sum1.spread(factor)

        regular_backward(
            (4, 5), qkvt_ref.at[w], kv_ref.at[w], e_ref.at[w], r_ref.at[w], o_ref.at[w],
            da_ref.at[w], dqkvt_ref.at[w],
        )
        total_ref[0, 512:704] += dot(dqkvt_ref[w, FIRST:], nb_ref[w])

    loop(0, 4, last_heads)
    sumb.start()

    def result(w):
        return pltpu.make_async_copy(
            x32_ref.at[:, :, columns(w), :], out_ref.at[:, :, columns(w), :], osem.at[w]
        )

    def input_gradient(w):
        @pl.when(w == 2)
        def _():
            suma.middle()

        d_normed = dot(wp_ref[0], dqkvt_ref[w]).T
        out = gb_ref[w].astype(F32) + norm_back(d_normed, normed_ref[w], inv_ref[w], gain_ref[0:1])
        x32_ref[:, :, columns(w), :] = out.reshape(WIN, WIN, WIN, C)
        result(w).start()

    loop(0, 4, input_gradient)
    sumb.middle()
    suma.spread(factor)
    for halo in (cot, middle, back):
        halo.finish()
    sum1.finish(res1_ref)
    sum1.drain()
    sumb.spread(factor)
    loop(0, 4, lambda w: result(w).wait())
    suma.finish(resa_ref)
    suma.drain()
    sumb.finish(resb_ref)
    sumb.drain()


def add_projection(total, attended_t, g_b):
    sums = dot(attended_t, g_b)
    total[FIRST:512] += sums[:128]
    total[704:768] += sums[128:]


def deliver(
    raw_ref, res1_ref, resa_ref, resb_ref, gain_ref, w_ref, out_ref, ggain_ref, gqkv_ref, gproj_ref,
    held, sem,
):
    loads = [pltpu.make_async_copy(raw_ref.at[d], held.at[d], sem.at[0, d]) for d in range(WIN)]
    copies = [pltpu.make_async_copy(held.at[d], out_ref.at[d], sem.at[1, d]) for d in range(WIN)]
    for load in loads:
        load.start()
    for load, copy in zip(loads, copies):
        load.wait()
        copy.start()
    pieces = [
        [resa_ref[...].astype(F32), resb_ref[...].astype(F32)],
        [res1_ref[slice(*p)].astype(F32) for p in PIECES],
    ]
    for block, (a, b) in enumerate(pieces):
        order = (a[:128], b[:64], a[128:256], b[64:128], a[256:FIRST], b[128:C])
        sums = jnp.concatenate(order, axis=0).T
        gqkv_ref[block] = sums
        gproj_ref[block] = jnp.concatenate([a[FIRST:], b[C:]], axis=0)
        gain = jnp.sum((w_ref[block].astype(F32) * sums).T, axis=0, keepdims=True)
        ggain_ref[block : block + 1] = gain / gain_ref[block : block + 1]
    for copy in copies:
        copy.wait()


def local(tokens, cotangent, gains, qkv_weight, proj_weight):
    depth_count, row_count, col_count, features = tokens.shape
    ny, nx = lax.axis_size("gy"), lax.axis_size("gx")
    factor = (depth_count * row_count * col_count * ny * nx // 16) ** (-0.5)
    whole = pl.BlockSpec(memory_space=pltpu.VMEM)
    anywhere = pl.BlockSpec(memory_space=pl.ANY)
    grad_shape = jax.ShapeDtypeStruct((WIN, WIN, 32, C), F32)
    counts = (768, 512, 256)
    nxx, nlow, nz = sizes_of(ny, nx)
    n1, n2 = nxx * nz, 4 * nlow
    scratch = [
        ((WIN, WIN, 32, C), F32),
        ((2, 3 * C, C), BF16),
        ((2, C, 3 * C), BF16),
        ((2, C, 2 * C), BF16),
        ((C, C), BF16),
        ((2, HALF, HALF), F32),
        ((4, HEADS, TOK, TOK), BF16),
        ((4, 8, TOK), F32),
        ((4, C, TOK), F32),
        ((4, 3 * C, TOK), BF16),
        ((4, TOK, 2 * C), BF16),
        ((4, TOK, C), BF16),
        ((4, TOK, C), F32),
        ((4, TOK, 1), F32),
        ((3 * C, TOK), BF16),
        ((TOK, 2 * C), BF16),
        ((C, TOK), BF16),
        ((4, C, TOK), F32),
        ((4, 3 * C, TOK), BF16),
        ((4, TOK, C), BF16),
        ((2, 4 * C, C), F32),
        ((3, 4, WIN, 64, C), BF16),
        ((3, 5, WIN, 64, C), BF16),
        ((3, WIN, 32, C), BF16),
        ((3, WIN, 32, C), BF16),
    ]
    for count in counts:
        size = count // n1
        scratch += [((k, size, C), BF16) for k in (n1, n1, n2, n1)]
    sems = [(3, 6), (3, 6), (3, n1), (3, n1), (3, n2), (3, n2), (3, n1), (3, n1), (4,)]
    raw, res1, resa, resb = pl.pallas_call(
        functools.partial(kernel, factor),
        out_shape=[grad_shape] + [jax.ShapeDtypeStruct((count, C), BF16) for count in counts],
        in_specs=[whole] * 5,
        out_specs=[anywhere] + [whole] * 3,
        scratch_shapes=[pltpu.VMEM(*s) for s in scratch]
        + [pltpu.SemaphoreType.DMA(s) for s in sems],
        compiler_params=pltpu.CompilerParams(
            vmem_limit_bytes=60 * 2**20, collective_id=0, has_side_effects=True
        ),
    )(tokens, cotangent, gains, qkv_weight, proj_weight)
    outs = [((2, C), F32), ((2, C, 3 * C), F32), ((2, C, C), F32)]
    return pl.pallas_call(
        deliver,
        out_shape=[grad_shape] + [jax.ShapeDtypeStruct(*o) for o in outs],
        in_specs=[anywhere] + [whole] * 5,
        out_specs=[anywhere] + [whole] * 3,
        scratch_shapes=[
            pltpu.VMEM((WIN, WIN, 32, C), F32),
            pltpu.SemaphoreType.DMA((2, WIN)),
        ],
        compiler_params=pltpu.CompilerParams(vmem_limit_bytes=60 * 2**20),
    )(raw, res1, resa, resb, gains, qkv_weight)


def solution(mesh):
    in_specs = (P(None, "gy", "gx", None), P(None, "gy", "gx", None), P(), P(), P())
    out_specs = (P(None, "gy", "gx", None), P(), P(), P())
    return jax.shard_map(local, mesh=mesh, in_specs=in_specs, out_specs=out_specs, check_vma=False)
```
